512 devices in a mesh: blk: 16 (over x, y_hi, core), dp: 32 (over z, y_lo).
Axes of the slice: x: 4, y: 4 (y_hi: 2, y_lo: 2; y = y_hi * 2 + y_lo), z: 16, core: 2. Of those that a mesh axis runs over, the one named last changes fastest.
Arguments:
- inputs: bfloat16 [32768, 2048], P('dp'), may hold values from -6 to 6
- inducing: bfloat16 [2048, 2048], P('blk'), may hold values from -6 to 6
Outputs:
- gram_slab: float32 [2048, 2048], P(('blk', 'dp'))
The draws below stay inside these ranges and needn't reach their ends.
All inputs are finite; a program needn't handle non-finite values.
Results may differ from the reference program's by a relative error of at most 0.0003.
Values may be sent and summed in bfloat16 or wider, within the bound.
A program may use at most 64 MiB of HBM per device.

```python
import jax
import jax.numpy as jnp

FEAT = 2048
INDUCING = 2048
TOTAL = 32768


def block_levels(rng, dims, split, smallest, top_value):
    gain = 1.0
    for position, shards_of in split:
        draws = jax.random.uniform(jax.random.fold_in(jax.random.fold_in(rng, 6), position), (shards_of,), jnp.float32, smallest / len(split), top_value / len(split))
        gain = gain * jnp.repeat(jnp.exp(draws), dims[position] // shards_of).reshape((-1,) + (1,) * (len(dims) - 1 - position))
    return gain


def noise(own_key, dims, deviation, most, pieces=(), dtype=jnp.bfloat16):
    drawn = jax.random.normal(own_key, dims, jnp.float32) * deviation
    if len(pieces) > 0:
        drawn = block_levels(own_key, dims, pieces, -0.22, 0.18) * drawn
    return jnp.clip(drawn, min=-most, max=most).astype(dtype)


def setup_inputs(seed: int = 0) -> dict:
    arg_keys = jax.random.split(jax.random.key(seed), 3)
    return {
        "inputs": noise(arg_keys[0], (TOTAL, FEAT), 1.0, 6.0, ((0, 32),)),
        "inducing": noise(arg_keys[1], (INDUCING, FEAT), 1.0, 6.0, ((0, 16),)),
    }


def reference(inputs, inducing):
    products = jnp.dot(inputs, inducing.T, preferred_element_type=jnp.float32)
    kernel = (products * products * (1.0 / FEAT)).astype(jnp.bfloat16)
    summed = jnp.dot(kernel.T, kernel, preferred_element_type=jnp.float32)
    return summed * (1.0 / TOTAL)
```

```python
import jax
import jax.numpy as jnp
from jax import lax
from jax.experimental import pallas as pl
from jax.experimental.pallas import tpu as pltpu
from jax.sharding import PartitionSpec as P

ROWS = 1024
FEAT = 2048
BLOCK = 128
CHUNKS = 4
CHUNK = ROWS // CHUNKS
TOTAL = 32768
OWN, EDGE, SIDE, FAR = 0, 2, 4, 5


def kernel(
    inputs, inducing, out, x_buf, i_buf, pieces, tiles, parts, strips, landed,
    in_sem, send_k, recv_k, recv_e, send_e, send_a, recv_a, send_b, recv_b,
    round_c, round_h, round_l, round_x, round_z, round_w,
):
    blk, dp = lax.axis_index("blk"), lax.axis_index("dp")
    x, yh, c = blk // 4, blk // 2 % 2, blk % 2
    z, yl = dp // 2, dp % 2

    def block_of(x_, yh_, c_):
        return (x_ + 8) % 4 * 4 + yh_ * 2 + c_

    def group_of(z_, yl_):
        return (z_ + 32) % 16 * 2 + yl_

    def remote(src, dst, send, recv, device):
        return pltpu.make_async_remote_copy(
            src_ref=src, dst_ref=dst, send_sem=send, recv_sem=recv,
            device_id=device, device_id_type=pl.DeviceIdType.MESH,
        )

    def signal(sem, device):
        pl.semaphore_signal(sem, inc=1, device_id=device, device_id_type=pl.DeviceIdType.MESH)

    def wait_bytes(ref, sem):
        pltpu.make_async_copy(ref, ref, sem).wait()

    load_i = pltpu.make_async_copy(inducing, i_buf, in_sem.at[CHUNKS])
    load_i.start()
    loads = []
    for n in range(CHUNKS):
        rows = pl.ds(n * CHUNK, CHUNK)
        load = pltpu.make_async_copy(inputs.at[rows], x_buf.at[rows], in_sem.at[n])
        load.start()
        loads.append(load)

    partner = (block_of(x, yh, 1 - c), dp)
    edge = (block_of(x, 1 - yh, c), dp)
    beside = (blk, group_of(z, 1 - yl))
    line = [(block_of(x + s, yh, c), dp) for s in (1, 2, 3)]
    column = [(blk, group_of(z + s, l)) for s in (-2, -1, 1, 2) for l in (0, 1)]
    near = [partner, edge, beside] + line + column
    barrier = pltpu.get_barrier_semaphore()
    for device in near:
        signal(barrier, device)

    def make_chunk(n):
        rows = pl.ds(n * CHUNK, CHUNK)
        loads[n].wait()
        products = lax.dot_general(
            x_buf[rows, :], i_buf[...], (((1,), (1,)), ((), ())),
            preferred_element_type=jnp.float32,
        )
        pieces[OWN + c, rows, :] = (products * products * (1.0 / FEAT)).astype(jnp.bfloat16)

    def send_chunk(n):
        rows = pl.ds(n * CHUNK, CHUNK)
        own = pieces.at[OWN + c, rows]
        remote(own, pieces.at[OWN + c, rows], send_k, recv_k.at[0], partner).start()
        remote(own, pieces.at[EDGE + c, rows], send_k, recv_e.at[n], edge).start()
        remote(own, pieces.at[SIDE, rows], send_k, recv_k.at[1], line[2]).start()
        remote(own, pieces.at[FAR, rows], send_k, recv_k.at[2], line[1]).start()

    load_i.wait()
    make_chunk(0)
    pl.semaphore_wait(barrier, len(near))
    send_chunk(0)
    for n in range(1, CHUNKS):
        make_chunk(n)
        send_chunk(n)

    signal(round_c, partner)
    pl.semaphore_wait(round_c, 1)
    signal(round_h, edge)

    def gram(left, right):
        return lax.dot_general(
            pieces[left], pieces[right], (((0,), (0,)), ((), ())),
            preferred_element_type=jnp.float32,
        )

    def send_tile(k, place):
        reach = 1 + c
        step = (k % 4 - z + 16 + reach) % 4 - reach
        target = group_of(z + step, k // 4)
        slot = yl * 4 + step + reach
        src, dst = tiles.at[k if place == 0 else 8], parts.at[place, slot]

        @pl.when(target == dp)
        def _():
            pltpu.make_async_copy(src, dst, recv_a.at[place]).start()

        @pl.when(target != dp)
        def _():
            remote(src, dst, send_a.at[place], recv_a.at[place], (blk, target)).start()

    wait_bytes(pieces.at[0], recv_k.at[0])
    tiles[0] = gram(OWN + c, OWN)
    send_tile(0, 0)
    tiles[8] = gram(OWN + c, OWN + 1)
    send_tile(0, 1)

    pl.semaphore_wait(round_h, 1)
    signal(round_l, beside)

    for n in range(CHUNKS):
        rows = pl.ds(n * CHUNK, CHUNK)
        arrived = pieces.at[EDGE + c, rows]
        wait_bytes(arrived, recv_e.at[n])
        remote(arrived, arrived, send_e, recv_k.at[3], partner).start()
    tiles[5] = gram(EDGE + c, OWN + (c + yh) % 2)
    send_tile(5, 0)

    pl.semaphore_wait(round_l, 1)
    for device in line:
        signal(round_x, device)

    wait_bytes(pieces.at[0], recv_k.at[1])
    tiles[1] = gram(SIDE, OWN)
    send_tile(1, 0)
    tiles[2] = gram(SIDE, OWN + 1)
    send_tile(2, 0)

    pl.semaphore_wait(round_x, 3)
    for s in (-2, 2):
        signal(round_z, (blk, group_of(z + s, yl)))

    wait_bytes(pieces.at[0], recv_k.at[3])
    tiles[3] = gram(SIDE, EDGE)
    send_tile(3, 0)
    tiles[4] = gram(SIDE, EDGE + 1)
    send_tile(4, 0)

    pl.semaphore_wait(round_z, 2)
    for s in (-4, 4):
        signal(round_w, (blk, group_of(z + s, yl)))

    wait_bytes(pieces.at[0], recv_k.at[2])
    half = (c + x // 2) % 2
    tiles[6] = gram(FAR, OWN + half)
    send_tile(6, 0)
    tiles[7] = gram(FAR, EDGE + half)
    send_tile(7, 0)

    pl.semaphore_wait(round_w, 2)

    mine = yl * 4 + z % 4
    first = mine == 0

    def one(k, value):
        return jnp.where(mine == k, value, 0)

    own_0, own_1 = block_of(x, yh, 0), block_of(x, yh, 1)
    edge_0, edge_1 = block_of(x, 1 - yh, 0), block_of(x, 1 - yh, 1)
    side, far = block_of(x + 1, yh, c), block_of(x + 2, yh, c)
    row = (
        one(0, blk) + one(1, side) + one(2, side) + one(3, side) + one(4, side)
        + one(5, block_of(x, 1 - yh, c)) + one(6, far) + one(7, far)
    )
    col = (
        one(0, own_0) + one(1, own_0) + one(2, own_1) + one(3, edge_0) + one(4, edge_1)
        + one(5, block_of(x, yh, (c + yh) % 2)) + one(6, block_of(x, yh, half))
        + one(7, block_of(x, 1 - yh, half))
    )
    rows_of = (row, jnp.where(first, blk, col))
    cols_of = (col, jnp.where(first, own_1, row))

    def add_parts(place):
        total = parts[place, 0]
        for s in range(1, 8):
            total = total + parts[place, s]
        return total * (1.0 / TOTAL)

    def lay(place, value):
        for s in range(32):
            strips[place, s] = value[4 * s : 4 * s + 4]

    wait_bytes(parts.at[0], recv_a.at[0])
    tile = add_parts(0)
    lay(0, tile)

    @pl.when(first)
    def _():
        wait_bytes(parts.at[1], recv_a.at[1])
        lay(1, add_parts(1))

    @pl.when(jnp.logical_not(first))
    def _():
        lay(1, tile.T)

    def send_strips(n, carry):
        away = (8 - (n + 1) // 2) * (2 * (n % 2) - 1)
        w = (z + away + 32) % 16
        for l in (0, 1):
            for r in (0, 1):
                src = strips.at[r, w * 2 + l]
                dst = landed.at[z // 4 * 16 + cols_of[r]]
                target = w * 2 + l
                here = jnp.logical_and(target == dp, rows_of[r] == blk)

                @pl.when(here)
                def _():
                    pltpu.make_async_copy(src, dst, recv_b).start()

                @pl.when(jnp.logical_not(here))
                def _():
                    remote(src, dst, send_b.at[r], recv_b, (rows_of[r], target)).start()

        return carry

    lax.fori_loop(0, 16, send_strips, 0)

    wait_bytes(landed, recv_b)
    for g in range(16):
        out[:, g * BLOCK : (g + 1) * BLOCK] = (
            landed[g] + landed[16 + g] + landed[32 + g] + landed[48 + g]
        )

    wait_bytes(pieces.at[pl.ds(0, 4)], send_k)
    wait_bytes(pieces.at[0], send_e)
    wait_bytes(tiles.at[pl.ds(0, 7)], send_a.at[0])

    @pl.when(jnp.logical_not(first))
    def _():
        wait_bytes(tiles.at[0], send_a.at[1])

    for r in (0, 1):
        inside = rows_of[r] == blk

        @pl.when(inside)
        def _():
            wait_bytes(landed.at[pl.ds(0, 31)], send_b.at[r])

        @pl.when(jnp.logical_not(inside))
        def _():
            wait_bytes(landed.at[pl.ds(0, 32)], send_b.at[r])


def local(inputs, inducing):
    dma = pltpu.SemaphoreType.DMA
    regular = pltpu.SemaphoreType.REGULAR
    return pl.pallas_call(
        kernel,
        out_shape=jax.ShapeDtypeStruct((4, FEAT), jnp.float32),
        in_specs=[pl.BlockSpec(memory_space=pl.ANY)] * 2,
        out_specs=pl.BlockSpec(memory_space=pltpu.VMEM),
        scratch_shapes=[
            pltpu.VMEM((ROWS, FEAT), jnp.bfloat16),
            pltpu.VMEM((BLOCK, FEAT), jnp.bfloat16),
            pltpu.VMEM((6, ROWS, BLOCK), jnp.bfloat16),
            pltpu.VMEM((9, BLOCK, BLOCK), jnp.float32),
            pltpu.VMEM((2, 8, BLOCK, BLOCK), jnp.float32),
            pltpu.VMEM((2, 32, 4, BLOCK), jnp.float32),
            pltpu.VMEM((64, 4, BLOCK), jnp.float32),
            dma((CHUNKS + 1,)),
            dma,
            dma((4,)),
            dma((CHUNKS,)),
            dma,
            dma((2,)),
            dma((2,)),
            dma((2,)),
            dma,
            regular,
            regular,
            regular,
            regular,
            regular,
            regular,
        ],
        compiler_params=pltpu.CompilerParams(
            collective_id=0, has_side_effects=True, vmem_limit_bytes=48 * 1024 * 1024
        ),
    )(inputs, inducing)


def solution(mesh):
    placed = (P("dp", None), P("blk", None))
    return jax.shard_map(
        local, mesh=mesh, in_specs=placed, out_specs=P(("blk", "dp"), None), check_vma=False
    )
```

```python
import jax
import jax.numpy as jnp
from jax import lax
from jax.experimental import pallas as pl
from jax.experimental.pallas import tpu as pltpu
from jax.sharding import PartitionSpec as P

ROWS = 1024
FEAT = 2048
BLOCK = 128
CUTS = (0, 128, 384, 704, 1024)
CHUNKS = len(CUTS) - 1
TOTAL = 32768
OWN, EDGE, SIDE, FAR = 0, 2, 4, 5


def kernel(
    inputs, inducing, out, x_buf, i_buf, pieces, tiles, parts, strips, landed,
    in_sem, send_k, recv_k, recv_e, send_e, send_a, recv_a, send_b, recv_b,
    round_p, round_z, round_w,
):
    blk, dp = lax.axis_index("blk"), lax.axis_index("dp")
    x, yh, c = blk // 4, blk // 2 % 2, blk % 2
    z, yl = dp // 2, dp % 2

    def block_of(x_, yh_, c_):
        return (x_ + 8) % 4 * 4 + yh_ * 2 + c_

    def group_of(z_, yl_):
        return (z_ + 32) % 16 * 2 + yl_

    def remote(src, dst, send, recv, device):
        return pltpu.make_async_remote_copy(
            src_ref=src, dst_ref=dst, send_sem=send, recv_sem=recv,
            device_id=device, device_id_type=pl.DeviceIdType.MESH,
        )

    def signal(sem, device):
        pl.semaphore_signal(sem, inc=1, device_id=device, device_id_type=pl.DeviceIdType.MESH)

    def wait_bytes(ref, sem):
        pltpu.make_async_copy(ref, ref, sem).wait()

    load_i = pltpu.make_async_copy(inducing, i_buf, in_sem.at[CHUNKS])
    load_i.start()
    loads = []
    for n in range(CHUNKS):
        rows = pl.ds(CUTS[n], CUTS[n + 1] - CUTS[n])
        load = pltpu.make_async_copy(inputs.at[rows], x_buf.at[rows], in_sem.at[n])
        load.start()
        loads.append(load)

    partner = (block_of(x, yh, 1 - c), dp)
    edge = (block_of(x, 1 - yh, c), dp)
    across = (block_of(x, 1 - yh, 1 - c), dp)
    beside = (blk, group_of(z, 1 - yl))
    line = [(block_of(x + s, yh, c), dp) for s in (1, 2, 3)]
    column = [(blk, group_of(z + s, l)) for s in (-2, -1, 1, 2) for l in (0, 1)]
    plane = [partner, edge, across] + line
    near = plane + [beside] + column
    barrier = pltpu.get_barrier_semaphore()
    for device in near:
        signal(barrier, device)

    def make_chunk(n):
        rows = pl.ds(CUTS[n], CUTS[n + 1] - CUTS[n])
        loads[n].wait()
        products = lax.dot_general(
            x_buf[rows, :], i_buf[...], (((1,), (1,)), ((), ())),
            preferred_element_type=jnp.float32,
        )
        pieces[OWN + c, rows, :] = (products * products * (1.0 / FEAT)).astype(jnp.bfloat16)

    def send_chunk(n):
        rows = pl.ds(CUTS[n], CUTS[n + 1] - CUTS[n])
        own = pieces.at[OWN + c, rows]
        remote(own, pieces.at[OWN + c, rows], send_k.at[0], recv_k.at[0], partner).start()
        remote(own, pieces.at[SIDE, rows], send_k.at[1], recv_k.at[1], line[2]).start()
        remote(own, pieces.at[EDGE + c, rows], send_k.at[2], recv_e.at[n], edge).start()

        @pl.when(x % 2 == 0)
        def _():
            remote(own, pieces.at[FAR, rows], send_k.at[3], recv_k.at[2], line[1]).start()

    def send_far():
        wait_bytes(pieces.at[0], send_k.at[1])
        remote(pieces.at[OWN + c], pieces.at[FAR], send_k.at[3], recv_k.at[2], line[1]).start()

    load_i.wait()
    make_chunk(0)
    pl.semaphore_wait(barrier, len(near))
    send_chunk(0)
    for device in plane:
        signal(round_p, device)
    for n in range(1, CHUNKS):
        make_chunk(n)
        send_chunk(n)

    pl.semaphore_wait(round_p, len(plane))
    for s in (-2, 2):
        signal(round_z, (blk, group_of(z + s, yl)))

    def gram(left, *rights):
        turned = pieces[left].T
        return [
            lax.dot_general(
                turned, pieces[right], (((1,), (0,)), ((), ())),
                preferred_element_type=jnp.float32,
            )
            for right in rights
        ]

    def send_tile(k, place):
        reach = 1 + c
        step = (k + 2 * c - z + 16 + reach) % 4 - reach
        target = group_of(z + step, (k // 4 + c) % 2)
        slot = yl * 4 + step + reach
        src, dst = tiles.at[k if place == 0 else 8], parts.at[place, slot]

        @pl.when(target == dp)
        def _():
            pltpu.make_async_copy(src, dst, recv_a.at[place]).start()

        @pl.when(target != dp)
        def _():
            remote(src, dst, send_a.at[place], recv_a.at[place], (blk, target)).start()

    wait_bytes(pieces.at[0], recv_k.at[0])
    tiles[0], tiles[8] = gram(OWN + c, OWN, OWN + 1)
    send_tile(0, 0)
    send_tile(0, 1)

    @pl.when(x % 2 == 1)
    def _():
        send_far()

    for n in range(CHUNKS):
        rows = pl.ds(CUTS[n], CUTS[n + 1] - CUTS[n])
        arrived = pieces.at[EDGE + c, rows]
        wait_bytes(arrived, recv_e.at[n])
        remote(arrived, arrived, send_e, recv_k.at[3], partner).start()

    pl.semaphore_wait(round_z, 2)
    for s in (-4, 4):
        signal(round_w, (blk, group_of(z + s, yl)))

    wait_bytes(pieces.at[0], recv_k.at[1])
    tiles[2], tiles[7] = gram(SIDE, OWN, OWN + 1)
    send_tile(2, 0)
    send_tile(7, 0)
    (tiles[5],) = gram(EDGE + c, OWN + (c + yh) % 2)
    send_tile(5, 0)

    wait_bytes(pieces.at[0], recv_k.at[3])
    tiles[4], tiles[1] = gram(SIDE, EDGE, EDGE + 1)
    send_tile(4, 0)
    send_tile(1, 0)

    wait_bytes(pieces.at[0], recv_k.at[2])
    half = (c + x // 2) % 2
    tiles[6], tiles[3] = gram(FAR, OWN + half, EDGE + half)
    send_tile(6, 0)
    send_tile(3, 0)

    pl.semaphore_wait(round_w, 2)

    mine = (yl + c) % 2 * 4 + (z + 2 * c) % 4
    first = mine == 0

    def one(k, value):
        return jnp.where(mine == k, value, 0)

    own_0, own_1 = block_of(x, yh, 0), block_of(x, yh, 1)
    edge_0, edge_1 = block_of(x, 1 - yh, 0), block_of(x, 1 - yh, 1)
    side, far = block_of(x + 1, yh, c), block_of(x + 2, yh, c)
    row = (
        one(0, blk) + one(2, side) + one(7, side) + one(4, side) + one(1, side)
        + one(5, block_of(x, 1 - yh, c)) + one(6, far) + one(3, far)
    )
    col = (
        one(0, own_0) + one(2, own_0) + one(7, own_1) + one(4, edge_0) + one(1, edge_1)
        + one(5, block_of(x, yh, (c + yh) % 2)) + one(6, block_of(x, yh, half))
        + one(3, block_of(x, 1 - yh, half))
    )
    rows_of = (row, jnp.where(first, blk, col))
    cols_of = (col, jnp.where(first, own_1, row))

    def add_parts(place):
        total = parts[place, 0]
        for s in range(1, 8):
            total = total + parts[place, s]
        return total * (1.0 / TOTAL)

    def lay(place, value):
        for s in range(32):
            strips[place, s] = value[4 * s : 4 * s + 4]

    wait_bytes(parts.at[0], recv_a.at[0])
    tile = add_parts(0)
    lay(0, tile)

    @pl.when(first)
    def _():
        wait_bytes(parts.at[1], recv_a.at[1])
        lay(1, add_parts(1))

    @pl.when(jnp.logical_not(first))
    def _():
        lay(1, tile.T)

    def send_strips(n, carry):
        w = n + n // 8 * (23 - 2 * n)
        for l in (0, 1):
            for r in (0, 1):
                src = strips.at[r, w * 2 + l]
                dst = landed.at[z // 4 * 16 + cols_of[r]]
                target = w * 2 + l
                here = jnp.logical_and(target == dp, rows_of[r] == blk)

                @pl.when(here)
                def _():
                    pltpu.make_async_copy(src, dst, recv_b).start()

                @pl.when(jnp.logical_not(here))
                def _():
                    remote(src, dst, send_b.at[r], recv_b, (rows_of[r], target)).start()

        return carry

    lax.fori_loop(0, 16, send_strips, 0)

    wait_bytes(landed, recv_b)
    for g in range(16):
        out[:, g * BLOCK : (g + 1) * BLOCK] = (
            landed[g] + landed[16 + g] + landed[32 + g] + landed[48 + g]
        )

    for n in (0, 2, 3):
        wait_bytes(pieces.at[0], send_k.at[n])

    @pl.when(x % 2 == 0)
    def _():
        wait_bytes(pieces.at[0], send_k.at[1])

    wait_bytes(pieces.at[0], send_e)
    wait_bytes(tiles.at[pl.ds(0, 7)], send_a.at[0])

    @pl.when(jnp.logical_not(first))
    def _():
        wait_bytes(tiles.at[0], send_a.at[1])

    for r in (0, 1):
        inside = rows_of[r] == blk

        @pl.when(inside)
        def _():
            wait_bytes(landed.at[pl.ds(0, 31)], send_b.at[r])

        @pl.when(jnp.logical_not(inside))
        def _():
            wait_bytes(landed.at[pl.ds(0, 32)], send_b.at[r])


def local(inputs, inducing):
    dma = pltpu.SemaphoreType.DMA
    regular = pltpu.SemaphoreType.REGULAR
    return pl.pallas_call(
        kernel,
        out_shape=jax.ShapeDtypeStruct((4, FEAT), jnp.float32),
        in_specs=[pl.BlockSpec(memory_space=pl.ANY)] * 2,
        out_specs=pl.BlockSpec(memory_space=pltpu.VMEM),
        scratch_shapes=[
            pltpu.VMEM((ROWS, FEAT), jnp.bfloat16),
            pltpu.VMEM((BLOCK, FEAT), jnp.bfloat16),
            pltpu.VMEM((6, ROWS, BLOCK), jnp.bfloat16),
            pltpu.VMEM((9, BLOCK, BLOCK), jnp.float32),
            pltpu.VMEM((2, 8, BLOCK, BLOCK), jnp.float32),
            pltpu.VMEM((2, 32, 4, BLOCK), jnp.float32),
            pltpu.VMEM((64, 4, BLOCK), jnp.float32),
            dma((CHUNKS + 1,)),
            dma((4,)),
            dma((4,)),
            dma((CHUNKS,)),
            dma,
            dma((2,)),
            dma((2,)),
            dma((2,)),
            dma,
            regular,
            regular,
            regular,
        ],
        compiler_params=pltpu.CompilerParams(
            collective_id=0, has_side_effects=True, vmem_limit_bytes=215 * 256 * 1024
        ),
    )(inputs, inducing)


def solution(mesh):
    placed = (P("dp", None), P("blk", None))
    return jax.shard_map(
        local, mesh=mesh, in_specs=placed, out_specs=P(("blk", "dp"), None), check_vma=False
    )
```

```python
import jax
import jax.numpy as jnp
from jax import lax
from jax.experimental import pallas as pl
from jax.experimental.pallas import tpu as pltpu
from jax.sharding import PartitionSpec as P

ROWS = 1024
FEAT = 2048
BLOCK = 128
CUTS = (0, 128, 384, 704, 1024)
CHUNKS = len(CUTS) - 1
TOTAL = 32768
OWN, EDGE, SIDE, FAR = 0, 2, 4, 5


def kernel(
    inputs, inducing, out, x_buf, i_buf, pieces, tiles, parts, sums, strips, landed,
    in_sem, send_k, recv_k, recv_e, send_e, send_a, recv_a, send_u, send_b, recv_b,
    round_p, round_z, round_w,
):
    blk, dp = lax.axis_index("blk"), lax.axis_index("dp")
    x, yh, c = blk // 4, blk // 2 % 2, blk % 2
    z, yl = dp // 2, dp % 2

    def block_of(x_, yh_, c_):
        return (x_ + 8) % 4 * 4 + yh_ * 2 + c_

    def group_of(z_, yl_):
        return (z_ + 32) % 16 * 2 + yl_

    def remote(src, dst, send, recv, device):
        return pltpu.make_async_remote_copy(
            src_ref=src, dst_ref=dst, send_sem=send, recv_sem=recv,
            device_id=device, device_id_type=pl.DeviceIdType.MESH,
        )

    def signal(sem, device):
        pl.semaphore_signal(sem, inc=1, device_id=device, device_id_type=pl.DeviceIdType.MESH)

    def wait_bytes(ref, sem):
        pltpu.make_async_copy(ref, ref, sem).wait()

    load_i = pltpu.make_async_copy(inducing, i_buf, in_sem.at[CHUNKS])
    load_i.start()
    loads = []
    for n in range(CHUNKS):
        rows = pl.ds(CUTS[n], CUTS[n + 1] - CUTS[n])
        load = pltpu.make_async_copy(inputs.at[rows], x_buf.at[rows], in_sem.at[n])
        load.start()
        loads.append(load)

    partner = (block_of(x, yh, 1 - c), dp)
    edge = (block_of(x, 1 - yh, c), dp)
    across = (block_of(x, 1 - yh, 1 - c), dp)
    beside = (blk, group_of(z, 1 - yl))
    line = [(block_of(x + s, yh, c), dp) for s in (1, 2, 3)]
    column = [(blk, group_of(z + s, l)) for s in (-2, -1, 1, 2) for l in (0, 1)]
    plane = [partner, edge, across] + line
    near = plane + [beside] + column
    barrier = pltpu.get_barrier_semaphore()
    for device in near:
        signal(barrier, device)

    def make_chunk(n):
        rows = pl.ds(CUTS[n], CUTS[n + 1] - CUTS[n])
        loads[n].wait()
        products = lax.dot_general(
            x_buf[rows, :], i_buf[...], (((1,), (1,)), ((), ())),
            preferred_element_type=jnp.float32,
        )
        pieces[OWN + c, rows, :] = (products * products * (1.0 / FEAT)).astype(jnp.bfloat16)

    def send_chunk(n):
        rows = pl.ds(CUTS[n], CUTS[n + 1] - CUTS[n])
        own = pieces.at[OWN + c, rows]
        remote(own, pieces.at[OWN + c, rows], send_k.at[0], recv_k.at[0], partner).start()
        remote(own, pieces.at[SIDE, rows], send_k.at[1], recv_k.at[1], line[2]).start()
        remote(own, pieces.at[EDGE + c, rows], send_k.at[2], recv_e.at[n], edge).start()

        @pl.when(x % 2 == 0)
        def _():
            remote(own, pieces.at[FAR, rows], send_k.at[3], recv_k.at[2], line[1]).start()

    def send_far():
        wait_bytes(pieces.at[0], send_k.at[1])
        remote(pieces.at[OWN + c], pieces.at[FAR], send_k.at[3], recv_k.at[2], line[1]).start()

    load_i.wait()
    make_chunk(0)
    pl.semaphore_wait(barrier, len(near))
    send_chunk(0)
    for device in plane:
        signal(round_p, device)
    for n in range(1, CHUNKS):
        make_chunk(n)
        send_chunk(n)

    pl.semaphore_wait(round_p, len(plane))
    for s in (-2, 2):
        signal(round_z, (blk, group_of(z + s, yl)))

    def gram(left, *rights):
        turned = pieces[left].T
        return [
            lax.dot_general(
                turned, pieces[right], (((1,), (0,)), ((), ())),
                preferred_element_type=jnp.float32,
            )
            for right in rights
        ]

    reach = 1 + c
    meets = (yl + c + 1) % 2
    middle = z % 4 == 2 * c

    def send_tile(k, place):
        step = (k + 2 * c - z + 16 + reach) % 4 - reach
        if k == 0:
            target = group_of(z + step, yl)
            dst = parts.at[meets * place + 1 - meets, (meets * yl + (1 - meets) * place) * 4 + step + reach]
            recv = recv_a.at[meets * place + (1 - meets) * 2]
        else:
            target = group_of(z + step, (k // 4 + c) % 2)
            dst, recv = parts.at[0, yl * 4 + step + reach], recv_a.at[0]
        src = tiles.at[8 if place else k]

        @pl.when(target == dp)
        def _():
            pltpu.make_async_copy(src, dst, recv).start()

        @pl.when(target != dp)
        def _():
            remote(src, dst, send_a.at[place], recv, (blk, target)).start()

    wait_bytes(pieces.at[0], recv_k.at[0])
    tiles[0], tiles[8] = gram(OWN + c, OWN, OWN + 1)
    send_tile(0, 0)
    send_tile(0, 1)

    @pl.when(x % 2 == 1)
    def _():
        send_far()

    for n in range(CHUNKS):
        rows = pl.ds(CUTS[n], CUTS[n + 1] - CUTS[n])
        arrived = pieces.at[EDGE + c, rows]
        wait_bytes(arrived, recv_e.at[n])
        remote(arrived, arrived, send_e, recv_k.at[3], partner).start()

    pl.semaphore_wait(round_z, 2)
    for s in (-4, 4):
        signal(round_w, (blk, group_of(z + s, yl)))

    wait_bytes(pieces.at[0], recv_k.at[1])
    tiles[2], tiles[7] = gram(SIDE, OWN, OWN + 1)
    send_tile(2, 0)
    send_tile(7, 0)
    (tiles[5],) = gram(EDGE + c, OWN + (c + yh) % 2)
    send_tile(5, 0)

    wait_bytes(pieces.at[0], recv_k.at[3])
    tiles[4], tiles[1] = gram(SIDE, EDGE, EDGE + 1)
    send_tile(4, 0)
    send_tile(1, 0)

    between = jnp.logical_and(middle, meets == 0)

    @pl.when(between)
    def _():
        wait_bytes(parts.at[1], recv_a.at[2])
        for place in (0, 1):
            sums[place] = (
                parts[1, place * 4] + parts[1, place * 4 + 1]
                + parts[1, place * 4 + 2] + parts[1, place * 4 + 3]
            )
            remote(
                sums.at[place], parts.at[place, (1 - c) * 4], send_u, recv_a.at[place], beside
            ).start()

    wait_bytes(pieces.at[0], recv_k.at[2])
    half = (c + x // 2) % 2
    tiles[6], tiles[3] = gram(FAR, OWN + half, EDGE + half)
    send_tile(6, 0)
    send_tile(3, 0)

    pl.semaphore_wait(round_w, 2)

    mine = (yl + c) % 2 * 4 + (z + 2 * c) % 4
    first = mine == 0

    def one(k, value):
        return jnp.where(mine == k, value, 0)

    own_0, own_1 = block_of(x, yh, 0), block_of(x, yh, 1)
    edge_0, edge_1 = block_of(x, 1 - yh, 0), block_of(x, 1 - yh, 1)
    side, far = block_of(x + 1, yh, c), block_of(x + 2, yh, c)
    row = (
        one(0, blk) + one(2, side) + one(7, side) + one(4, side) + one(1, side)
        + one(5, block_of(x, 1 - yh, c)) + one(6, far) + one(3, far)
    )
    col = (
        one(0, own_0) + one(2, own_0) + one(7, own_1) + one(4, edge_0) + one(1, edge_1)
        + one(5, block_of(x, yh, (c + yh) % 2)) + one(6, block_of(x, yh, half))
        + one(3, block_of(x, 1 - yh, half))
    )
    rows_of = (row, jnp.where(first, blk, col))
    cols_of = (col, jnp.where(first, own_1, row))

    def add_parts(place, slots):
        total = parts[place, slots[0]]
        for s in slots[1:]:
            total = total + parts[place, s]
        return total * (1.0 / TOTAL)

    def lay(place, value):
        for s in range(32):
            strips[place, s] = value[4 * s : 4 * s + 4]

    @pl.when(first)
    def _():
        for place in (0, 1):
            wait_bytes(parts.at[place, pl.ds(0, 5)], recv_a.at[place])
            lay(place, add_parts(place, [(1 - c) * 4] + [c * 4 + s for s in range(4)]))

    @pl.when(jnp.logical_not(first))
    def _():
        wait_bytes(parts.at[0], recv_a.at[0])
        tile = add_parts(0, range(8))
        lay(0, tile)
        lay(1, tile.T)

    def send_strips(n, carry):
        w = n + n // 8 * (23 - 2 * n)
        for l in (0, 1):
            for r in (0, 1):
                src = strips.at[r, w * 2 + l]
                dst = landed.at[z // 4 * 16 + cols_of[r]]
                target = w * 2 + l
                here = jnp.logical_and(target == dp, rows_of[r] == blk)

                @pl.when(here)
                def _():
                    pltpu.make_async_copy(src, dst, recv_b).start()

                @pl.when(jnp.logical_not(here))
                def _():
                    remote(src, dst, send_b.at[r], recv_b, (rows_of[r], target)).start()

        return carry

    lax.fori_loop(0, 16, send_strips, 0)

    wait_bytes(landed, recv_b)
    for g in range(16):
        out[:, g * BLOCK : (g + 1) * BLOCK] = (
            landed[g] + landed[16 + g] + landed[32 + g] + landed[48 + g]
        )

    for n in (0, 2, 3):
        wait_bytes(pieces.at[0], send_k.at[n])

    @pl.when(x % 2 == 0)
    def _():
        wait_bytes(pieces.at[0], send_k.at[1])

    wait_bytes(pieces.at[0], send_e)
    @pl.when(between)
    def _():
        wait_bytes(tiles.at[pl.ds(0, 6)], send_a.at[0])
        wait_bytes(sums, send_u)

    @pl.when(jnp.logical_not(between))
    def _():
        wait_bytes(tiles.at[pl.ds(0, 7)], send_a.at[0])

    @pl.when(jnp.logical_not(middle))
    def _():
        wait_bytes(tiles.at[0], send_a.at[1])

    for r in (0, 1):
        inside = rows_of[r] == blk

        @pl.when(inside)
        def _():
            wait_bytes(landed.at[pl.ds(0, 31)], send_b.at[r])

        @pl.when(jnp.logical_not(inside))
        def _():
            wait_bytes(landed.at[pl.ds(0, 32)], send_b.at[r])


def local(inputs, inducing):
    dma = pltpu.SemaphoreType.DMA
    regular = pltpu.SemaphoreType.REGULAR
    return pl.pallas_call(
        kernel,
        out_shape=jax.ShapeDtypeStruct((4, FEAT), jnp.float32),
        in_specs=[pl.BlockSpec(memory_space=pl.ANY)] * 2,
        out_specs=pl.BlockSpec(memory_space=pltpu.VMEM),
        scratch_shapes=[
            pltpu.VMEM((ROWS, FEAT), jnp.bfloat16),
            pltpu.VMEM((BLOCK, FEAT), jnp.bfloat16),
            pltpu.VMEM((6, ROWS, BLOCK), jnp.bfloat16),
            pltpu.VMEM((9, BLOCK, BLOCK), jnp.float32),
            pltpu.VMEM((2, 8, BLOCK, BLOCK), jnp.float32),
            pltpu.VMEM((2, BLOCK, BLOCK), jnp.float32),
            pltpu.VMEM((2, 32, 4, BLOCK), jnp.float32),
            pltpu.VMEM((64, 4, BLOCK), jnp.float32),
            dma((CHUNKS + 1,)),
            dma((4,)),
            dma((4,)),
            dma((CHUNKS,)),
            dma,
            dma((2,)),
            dma((3,)),
            dma,
            dma((2,)),
            dma,
            regular,
            regular,
            regular,
        ],
        compiler_params=pltpu.CompilerParams(
            collective_id=0, has_side_effects=True, vmem_limit_bytes=215 * 256 * 1024
        ),
    )(inputs, inducing)


def solution(mesh):
    placed = (P("dp", None), P("blk", None))
    return jax.shard_map(
        local, mesh=mesh, in_specs=placed, out_specs=P(("blk", "dp"), None), check_vma=False
    )
```

```python
import jax
import jax.numpy as jnp
from jax import lax
from jax.experimental import pallas as pl
from jax.experimental.pallas import tpu as pltpu
from jax.sharding import PartitionSpec as P

ROWS = 1024
FEAT = 2048
BLOCK = 128
CUTS = (0, 128, 256, 640, 1024)
CHUNKS = len(CUTS) - 1
PASSED = 2
HALF = CUTS[PASSED]
TOTAL = 32768
OWN, EDGE, SIDE, FAR = 0, 2, 4, 5


def kernel(
    inputs, inducing, out, x_buf, i_buf, pieces, passing, tiles, parts, sums, strips, landed,
    in_sem, send_k, recv_k, send_p, recv_p, recv_e, send_e, send_a, recv_a, send_u, send_b, recv_b,
    round_p, round_z, round_w,
):
    blk, dp = lax.axis_index("blk"), lax.axis_index("dp")
    x, yh, c = blk // 4, blk // 2 % 2, blk % 2
    z, yl = dp // 2, dp % 2

    def block_of(x_, yh_, c_):
        return (x_ + 8) % 4 * 4 + yh_ * 2 + c_

    def group_of(z_, yl_):
        return (z_ + 32) % 16 * 2 + yl_

    def remote(src, dst, send, recv, device):
        return pltpu.make_async_remote_copy(
            src_ref=src, dst_ref=dst, send_sem=send, recv_sem=recv,
            device_id=device, device_id_type=pl.DeviceIdType.MESH,
        )

    def signal(sem, device):
        pl.semaphore_signal(sem, inc=1, device_id=device, device_id_type=pl.DeviceIdType.MESH)

    def wait_bytes(ref, sem):
        pltpu.make_async_copy(ref, ref, sem).wait()

    load_i = pltpu.make_async_copy(inducing, i_buf, in_sem.at[CHUNKS])
    load_i.start()
    loads = []
    for n in range(CHUNKS):
        rows = pl.ds(CUTS[n], CUTS[n + 1] - CUTS[n])
        load = pltpu.make_async_copy(inputs.at[rows], x_buf.at[rows], in_sem.at[n])
        load.start()
        loads.append(load)

    partner = (block_of(x, yh, 1 - c), dp)
    edge = (block_of(x, 1 - yh, c), dp)
    across = (block_of(x, 1 - yh, 1 - c), dp)
    beside = (blk, group_of(z, 1 - yl))
    line = [(block_of(x + s, yh, c), dp) for s in (1, 2, 3)]
    column = [(blk, group_of(z + s, l)) for s in (-2, -1, 1, 2) for l in (0, 1)]
    plane = [partner, edge, across] + line
    near = plane + [beside] + column
    barrier = pltpu.get_barrier_semaphore()
    for device in near:
        signal(barrier, device)

    def make_chunk(n):
        rows = pl.ds(CUTS[n], CUTS[n + 1] - CUTS[n])
        loads[n].wait()
        products = lax.dot_general(
            x_buf[rows, :], i_buf[...], (((1,), (1,)), ((), ())),
            preferred_element_type=jnp.float32,
        )
        pieces[OWN + c, rows, :] = (products * products * (1.0 / FEAT)).astype(jnp.bfloat16)

    def send_chunk(n):
        rows = pl.ds(CUTS[n], CUTS[n + 1] - CUTS[n])
        own = pieces.at[OWN + c, rows]
        remote(own, pieces.at[OWN + c, rows], send_k.at[0], recv_k.at[0], partner).start()
        remote(own, pieces.at[SIDE, rows], send_k.at[1], recv_k.at[1], line[2]).start()
        remote(own, pieces.at[EDGE + c, rows], send_k.at[2], recv_e.at[n], edge).start()

        if n < PASSED:

            @pl.when(x % 2 == 1)
            def _():
                remote(own, passing.at[rows], send_p, recv_p.at[n], line[0]).start()

    def send_far():
        @pl.when(x % 2 == 0)
        def _():
            remote(pieces.at[OWN + c], pieces.at[FAR], send_k.at[3], recv_k.at[2], line[1]).start()
            for n in range(PASSED):
                rows = pl.ds(CUTS[n], CUTS[n + 1] - CUTS[n])
                wait_bytes(passing.at[rows], recv_p.at[n])
                remote(passing.at[rows], pieces.at[FAR, rows], send_p, recv_k.at[2], line[0]).start()

        @pl.when(x % 2 == 1)
        def _():
            wait_bytes(pieces.at[0], send_k.at[1])
            rows = pl.ds(HALF, ROWS - HALF)
            remote(
                pieces.at[OWN + c, rows], pieces.at[FAR, rows], send_k.at[3], recv_k.at[2], line[1]
            ).start()

    load_i.wait()
    make_chunk(0)
    pl.semaphore_wait(barrier, len(near))
    send_chunk(0)
    for device in plane:
        signal(round_p, device)
    for n in range(1, CHUNKS):
        make_chunk(n)
        send_chunk(n)

    pl.semaphore_wait(round_p, len(plane))
    for s in (-2, 2):
        signal(round_z, (blk, group_of(z + s, yl)))

    def gram(left, *rights):
        turned = pieces[left].T
        return [
            lax.dot_general(
                turned, pieces[right], (((1,), (0,)), ((), ())),
                preferred_element_type=jnp.float32,
            )
            for right in rights
        ]

    reach = 1 + c
    meets = (yl + c + 1) % 2
    middle = z % 4 == 2 * c

    def send_tile(k, place):
        step = (k + 2 * c - z + 16 + reach) % 4 - reach
        if k == 0:
            target = group_of(z + step, yl)
            dst = parts.at[meets * place + 1 - meets, (meets * yl + (1 - meets) * place) * 4 + step + reach]
            recv = recv_a.at[meets * place + (1 - meets) * 2]
        else:
            target = group_of(z + step, (k // 4 + c) % 2)
            dst, recv = parts.at[0, yl * 4 + step + reach], recv_a.at[0]
        src = tiles.at[8 if place else k]

        @pl.when(target == dp)
        def _():
            pltpu.make_async_copy(src, dst, recv).start()

        @pl.when(target != dp)
        def _():
            remote(src, dst, send_a.at[place], recv, (blk, target)).start()

    wait_bytes(pieces.at[0], recv_k.at[0])
    tiles[0], tiles[8] = gram(OWN + c, OWN, OWN + 1)
    send_tile(0, 0)
    send_tile(0, 1)

    send_far()

    for n in range(CHUNKS):
        rows = pl.ds(CUTS[n], CUTS[n + 1] - CUTS[n])
        arrived = pieces.at[EDGE + c, rows]
        wait_bytes(arrived, recv_e.at[n])
        remote(arrived, arrived, send_e, recv_k.at[3], partner).start()

    pl.semaphore_wait(round_z, 2)
    for s in (-4, 4):
        signal(round_w, (blk, group_of(z + s, yl)))

    wait_bytes(pieces.at[0], recv_k.at[1])
    tiles[2], tiles[7] = gram(SIDE, OWN, OWN + 1)
    send_tile(2, 0)
    send_tile(7, 0)
    (tiles[5],) = gram(EDGE + c, OWN + (c + yh) % 2)
    send_tile(5, 0)

    wait_bytes(pieces.at[0], recv_k.at[3])
    tiles[4], tiles[1] = gram(SIDE, EDGE, EDGE + 1)
    send_tile(4, 0)
    send_tile(1, 0)

    between = jnp.logical_and(middle, meets == 0)

    @pl.when(between)
    def _():
        wait_bytes(parts.at[1], recv_a.at[2])
        for place in (0, 1):
            sums[place] = (
                parts[1, place * 4] + parts[1, place * 4 + 1]
                + parts[1, place * 4 + 2] + parts[1, place * 4 + 3]
            )
            remote(
                sums.at[place], parts.at[place, (1 - c) * 4], send_u, recv_a.at[place], beside
            ).start()

    wait_bytes(pieces.at[0], recv_k.at[2])
    half = (c + x // 2) % 2
    tiles[6], tiles[3] = gram(FAR, OWN + half, EDGE + half)
    send_tile(6, 0)
    send_tile(3, 0)

    pl.semaphore_wait(round_w, 2)

    mine = (yl + c) % 2 * 4 + (z + 2 * c) % 4
    first = mine == 0

    def one(k, value):
        return jnp.where(mine == k, value, 0)

    own_0, own_1 = block_of(x, yh, 0), block_of(x, yh, 1)
    edge_0, edge_1 = block_of(x, 1 - yh, 0), block_of(x, 1 - yh, 1)
    side, far = block_of(x + 1, yh, c), block_of(x + 2, yh, c)
    row = (
        one(0, blk) + one(2, side) + one(7, side) + one(4, side) + one(1, side)
        + one(5, block_of(x, 1 - yh, c)) + one(6, far) + one(3, far)
    )
    col = (
        one(0, own_0) + one(2, own_0) + one(7, own_1) + one(4, edge_0) + one(1, edge_1)
        + one(5, block_of(x, yh, (c + yh) % 2)) + one(6, block_of(x, yh, half))
        + one(3, block_of(x, 1 - yh, half))
    )
    rows_of = (row, jnp.where(first, blk, col))
    cols_of = (col, jnp.where(first, own_1, row))

    def add_parts(place, slots):
        total = parts[place, slots[0]]
        for s in slots[1:]:
            total = total + parts[place, s]
        return total * (1.0 / TOTAL)

    def lay(place, value):
        for s in range(32):
            strips[place, s] = value[4 * s : 4 * s + 4]

    @pl.when(first)
    def _():
        for place in (0, 1):
            wait_bytes(parts.at[place, pl.ds(0, 5)], recv_a.at[place])
            lay(place, add_parts(place, [(1 - c) * 4] + [c * 4 + s for s in range(4)]))

    @pl.when(jnp.logical_not(first))
    def _():
        wait_bytes(parts.at[0], recv_a.at[0])
        tile = add_parts(0, range(8))
        lay(0, tile)
        lay(1, tile.T)

    def send_strips(n, carry):
        w = n + n // 8 * (23 - 2 * n)
        for l in (0, 1):
            for r in (0, 1):
                src = strips.at[r, w * 2 + l]
                dst = landed.at[z // 4 * 16 + cols_of[r]]
                target = w * 2 + l
                here = jnp.logical_and(target == dp, rows_of[r] == blk)

                @pl.when(here)
                def _():
                    pltpu.make_async_copy(src, dst, recv_b).start()

                @pl.when(jnp.logical_not(here))
                def _():
                    remote(src, dst, send_b.at[r], recv_b, (rows_of[r], target)).start()

        return carry

    lax.fori_loop(0, 16, send_strips, 0)

    wait_bytes(landed, recv_b)
    for g in range(16):
        out[:, g * BLOCK : (g + 1) * BLOCK] = (
            landed[g] + landed[16 + g] + landed[32 + g] + landed[48 + g]
        )

    for n in (0, 2):
        wait_bytes(pieces.at[0], send_k.at[n])
    wait_bytes(passing, send_p)

    @pl.when(x % 2 == 0)
    def _():
        wait_bytes(pieces.at[0], send_k.at[1])
        wait_bytes(pieces.at[0], send_k.at[3])

    @pl.when(x % 2 == 1)
    def _():
        wait_bytes(pieces.at[0, pl.ds(HALF, ROWS - HALF)], send_k.at[3])

    wait_bytes(pieces.at[0], send_e)
    @pl.when(between)
    def _():
        wait_bytes(tiles.at[pl.ds(0, 6)], send_a.at[0])
        wait_bytes(sums, send_u)

    @pl.when(jnp.logical_not(between))
    def _():
        wait_bytes(tiles.at[pl.ds(0, 7)], send_a.at[0])

    @pl.when(jnp.logical_not(middle))
    def _():
        wait_bytes(tiles.at[0], send_a.at[1])

    for r in (0, 1):
        inside = rows_of[r] == blk

        @pl.when(inside)
        def _():
            wait_bytes(landed.at[pl.ds(0, 31)], send_b.at[r])

        @pl.when(jnp.logical_not(inside))
        def _():
            wait_bytes(landed.at[pl.ds(0, 32)], send_b.at[r])


def local(inputs, inducing):
    dma = pltpu.SemaphoreType.DMA
    regular = pltpu.SemaphoreType.REGULAR
    return pl.pallas_call(
        kernel,
        out_shape=jax.ShapeDtypeStruct((4, FEAT), jnp.float32),
        in_specs=[pl.BlockSpec(memory_space=pl.ANY)] * 2,
        out_specs=pl.BlockSpec(memory_space=pltpu.VMEM),
        scratch_shapes=[
            pltpu.VMEM((ROWS, FEAT), jnp.bfloat16),
            pltpu.VMEM((BLOCK, FEAT), jnp.bfloat16),
            pltpu.VMEM((6, ROWS, BLOCK), jnp.bfloat16),
            pltpu.VMEM((HALF, BLOCK), jnp.bfloat16),
            pltpu.VMEM((9, BLOCK, BLOCK), jnp.float32),
            pltpu.VMEM((2, 8, BLOCK, BLOCK), jnp.float32),
            pltpu.VMEM((2, BLOCK, BLOCK), jnp.float32),
            pltpu.VMEM((2, 32, 4, BLOCK), jnp.float32),
            pltpu.VMEM((64, 4, BLOCK), jnp.float32),
            dma((CHUNKS + 1,)),
            dma((4,)),
            dma((4,)),
            dma,
            dma((PASSED,)),
            dma((CHUNKS,)),
            dma,
            dma((2,)),
            dma((3,)),
            dma,
            dma((2,)),
            dma,
            regular,
            regular,
            regular,
        ],
        compiler_params=pltpu.CompilerParams(
            collective_id=0, has_side_effects=True, vmem_limit_bytes=215 * 256 * 1024
        ),
    )(inputs, inducing)


def solution(mesh):
    placed = (P("dp", None), P("blk", None))
    return jax.shard_map(
        local, mesh=mesh, in_specs=placed, out_specs=P(("blk", "dp"), None), check_vma=False
    )
```

```python
import jax
import jax.numpy as jnp
from jax import lax
from jax.experimental import pallas as pl
from jax.experimental.pallas import tpu as pltpu
from jax.sharding import PartitionSpec as P

ROWS = 1024
FEAT = 2048
BLOCK = 128
CUTS = (0, 128, 256, 640, 1024)
CHUNKS = len(CUTS) - 1
PASSED = 2
HALF = CUTS[PASSED]
TOTAL = 32768
OWN, EDGE, SIDE, FAR = 0, 2, 4, 5


def kernel(
    inputs, inducing, out, x_buf, i_buf, pieces, passing, tiles, parts, sums, strips, landed,
    in_sem, send_k, recv_k, send_p, recv_p, recv_e, send_e, send_a, recv_a, send_u, send_b, recv_b,
    round_p, round_z, round_w,
):
    blk, dp = lax.axis_index("blk"), lax.axis_index("dp")
    x, yh, c = blk // 4, blk // 2 % 2, blk % 2
    z, yl = dp // 2, dp % 2

    def block_of(x_, yh_, c_):
        return (x_ + 8) % 4 * 4 + yh_ * 2 + c_

    def group_of(z_, yl_):
        return (z_ + 32) % 16 * 2 + yl_

    def remote(src, dst, send, recv, device):
        return pltpu.make_async_remote_copy(
            src_ref=src, dst_ref=dst, send_sem=send, recv_sem=recv,
            device_id=device, device_id_type=pl.DeviceIdType.MESH,
        )

    def signal(sem, device):
        pl.semaphore_signal(sem, inc=1, device_id=device, device_id_type=pl.DeviceIdType.MESH)

    def wait_bytes(ref, sem):
        pltpu.make_async_copy(ref, ref, sem).wait()

    partner = (block_of(x, yh, 1 - c), dp)
    edge = (block_of(x, 1 - yh, c), dp)
    across = (block_of(x, 1 - yh, 1 - c), dp)
    beside = (blk, group_of(z, 1 - yl))
    line = [(block_of(x + s, yh, c), dp) for s in (1, 2, 3)]
    column = [(blk, group_of(z + s, l)) for s in (-2, -1, 1, 2) for l in (0, 1)]
    plane = [partner, edge, across] + line
    near = plane + [beside] + column
    barrier = pltpu.get_barrier_semaphore()
    for device in near:
        signal(barrier, device)

    load_i = pltpu.make_async_copy(inducing, i_buf, in_sem.at[CHUNKS])
    load_i.start()
    loads = []
    for n in range(CHUNKS):
        rows = pl.ds(CUTS[n], CUTS[n + 1] - CUTS[n])
        load = pltpu.make_async_copy(inputs.at[rows], x_buf.at[rows], in_sem.at[n])
        load.start()
        loads.append(load)

    def make_chunk(n):
        rows = pl.ds(CUTS[n], CUTS[n + 1] - CUTS[n])
        loads[n].wait()
        products = lax.dot_general(
            x_buf[rows, :], i_buf[...], (((1,), (1,)), ((), ())),
            preferred_element_type=jnp.float32,
        )
        pieces[OWN + c, rows, :] = (products * products * (1.0 / FEAT)).astype(jnp.bfloat16)

    def send_chunk(n):
        rows = pl.ds(CUTS[n], CUTS[n + 1] - CUTS[n])
        own = pieces.at[OWN + c, rows]
        remote(own, pieces.at[OWN + c, rows], send_k.at[0], recv_k.at[0], partner).start()
        remote(own, pieces.at[SIDE, rows], send_k.at[1], recv_k.at[1], line[2]).start()
        remote(own, pieces.at[EDGE + c, rows], send_k.at[2], recv_e.at[n], edge).start()

        if n < PASSED:

            @pl.when(x % 2 == 1)
            def _():
                remote(own, passing.at[rows], send_p, recv_p.at[n], line[0]).start()

    def send_far():
        @pl.when(x % 2 == 0)
        def _():
            remote(pieces.at[OWN + c], pieces.at[FAR], send_k.at[3], recv_k.at[2], line[1]).start()
            for n in range(PASSED):
                rows = pl.ds(CUTS[n], CUTS[n + 1] - CUTS[n])
                wait_bytes(passing.at[rows], recv_p.at[n])
                remote(passing.at[rows], pieces.at[FAR, rows], send_p, recv_k.at[2], line[0]).start()

        @pl.when(x % 2 == 1)
        def _():
            wait_bytes(pieces.at[0], send_k.at[1])
            rows = pl.ds(HALF, ROWS - HALF)
            remote(
                pieces.at[OWN + c, rows], pieces.at[FAR, rows], send_k.at[3], recv_k.at[2], line[1]
            ).start()

    load_i.wait()
    for n in range(1):
        make_chunk(n)
    pl.semaphore_wait(barrier, len(near))
    for n in range(CHUNKS):
        if n >= 1:
            make_chunk(n)
        send_chunk(n)
    for device in plane:
        signal(round_p, device)

    def gram(left, *rights):
        turned = pieces[left].T
        return [
            lax.dot_general(
                turned, pieces[right], (((1,), (0,)), ((), ())),
                preferred_element_type=jnp.float32,
            )
            for right in rights
        ]

    reach = 1 + c
    meets = (yl + c + 1) % 2
    middle = z % 4 == 2 * c

    def send_tile(k, place):
        step = (k + 2 * c - z + 16 + reach) % 4 - reach
        if k == 0:
            target = group_of(z + step, yl)
            dst = parts.at[meets * place + 1 - meets, (meets * yl + (1 - meets) * place) * 4 + step + reach]
            recv = recv_a.at[meets * place + (1 - meets) * 2]
        else:
            target = group_of(z + step, (k // 4 + c) % 2)
            dst, recv = parts.at[0, yl * 4 + step + reach], recv_a.at[0]
        src = tiles.at[8 if place else k]

        @pl.when(target == dp)
        def _():
            pltpu.make_async_copy(src, dst, recv).start()

        @pl.when(target != dp)
        def _():
            remote(src, dst, send_a.at[place], recv, (blk, target)).start()

    wait_bytes(pieces.at[0], recv_k.at[0])
    tiles[0], tiles[8] = gram(OWN + c, OWN, OWN + 1)
    send_tile(0, 0)
    send_tile(0, 1)

    send_far()

    pl.semaphore_wait(round_p, len(plane))
    for s in (-2, 2):
        signal(round_z, (blk, group_of(z + s, yl)))

    for n in range(CHUNKS):
        rows = pl.ds(CUTS[n], CUTS[n + 1] - CUTS[n])
        arrived = pieces.at[EDGE + c, rows]
        wait_bytes(arrived, recv_e.at[n])
        remote(arrived, arrived, send_e, recv_k.at[3], partner).start()

    pl.semaphore_wait(round_z, 2)
    for s in (-4, 4):
        signal(round_w, (blk, group_of(z + s, yl)))

    wait_bytes(pieces.at[0], recv_k.at[1])
    tiles[2], tiles[7] = gram(SIDE, OWN, OWN + 1)
    send_tile(2, 0)
    send_tile(7, 0)
    (tiles[5],) = gram(EDGE + c, OWN + (c + yh) % 2)
    send_tile(5, 0)

    wait_bytes(pieces.at[0], recv_k.at[3])
    tiles[4], tiles[1] = gram(SIDE, EDGE, EDGE + 1)
    send_tile(4, 0)
    send_tile(1, 0)

    between = jnp.logical_and(middle, meets == 0)

    @pl.when(between)
    def _():
        wait_bytes(parts.at[1], recv_a.at[2])
        for place in (0, 1):
            sums[place] = (
                parts[1, place * 4] + parts[1, place * 4 + 1]
                + parts[1, place * 4 + 2] + parts[1, place * 4 + 3]
            )
            remote(
                sums.at[place], parts.at[place, (1 - c) * 4], send_u, recv_a.at[place], beside
            ).start()

    wait_bytes(pieces.at[0], recv_k.at[2])
    half = (c + x // 2) % 2
    tiles[6], tiles[3] = gram(FAR, OWN + half, EDGE + half)
    send_tile(6, 0)
    send_tile(3, 0)

    pl.semaphore_wait(round_w, 2)

    mine = (yl + c) % 2 * 4 + (z + 2 * c) % 4
    first = mine == 0

    def one(k, value):
        return jnp.where(mine == k, value, 0)

    own_0, own_1 = block_of(x, yh, 0), block_of(x, yh, 1)
    edge_0, edge_1 = block_of(x, 1 - yh, 0), block_of(x, 1 - yh, 1)
    side, far = block_of(x + 1, yh, c), block_of(x + 2, yh, c)
    row = (
        one(0, blk) + one(2, side) + one(7, side) + one(4, side) + one(1, side)
        + one(5, block_of(x, 1 - yh, c)) + one(6, far) + one(3, far)
    )
    col = (
        one(0, own_0) + one(2, own_0) + one(7, own_1) + one(4, edge_0) + one(1, edge_1)
        + one(5, block_of(x, yh, (c + yh) % 2)) + one(6, block_of(x, yh, half))
        + one(3, block_of(x, 1 - yh, half))
    )
    rows_of = (row, jnp.where(first, blk, col))
    cols_of = (col, jnp.where(first, own_1, row))

    def add_parts(place, slots):
        total = parts[place, slots[0]]
        for s in slots[1:]:
            total = total + parts[place, s]
        return total * (1.0 / TOTAL)

    def lay(place, value):
        for s in range(32):
            strips[place, s] = value[4 * s : 4 * s + 4]

    @pl.when(first)
    def _():
        for place in (0, 1):
            wait_bytes(parts.at[place, pl.ds(0, 5)], recv_a.at[place])
            lay(place, add_parts(place, [(1 - c) * 4] + [c * 4 + s for s in range(4)]))

    @pl.when(jnp.logical_not(first))
    def _():
        wait_bytes(parts.at[0], recv_a.at[0])
        tile = add_parts(0, range(8))
        lay(0, tile)
        lay(1, tile.T)

    def send_strips(n, carry):
        w = n + n // 8 * (23 - 2 * n)
        for l in (0, 1):
            for r in (0, 1):
                src = strips.at[r, w * 2 + l]
                dst = landed.at[z // 4 * 16 + cols_of[r]]
                target = w * 2 + l
                here = jnp.logical_and(target == dp, rows_of[r] == blk)

                @pl.when(here)
                def _():
                    pltpu.make_async_copy(src, dst, recv_b).start()

                @pl.when(jnp.logical_not(here))
                def _():
                    remote(src, dst, send_b.at[r], recv_b, (rows_of[r], target)).start()

        return carry

    lax.fori_loop(0, 16, send_strips, 0)

    wait_bytes(landed, recv_b)
    for g in range(16):
        out[:, g * BLOCK : (g + 1) * BLOCK] = (
            landed[g] + landed[16 + g] + landed[32 + g] + landed[48 + g]
        )

    for n in (0, 2):
        wait_bytes(pieces.at[0], send_k.at[n])
    wait_bytes(passing, send_p)

    @pl.when(x % 2 == 0)
    def _():
        wait_bytes(pieces.at[0], send_k.at[1])
        wait_bytes(pieces.at[0], send_k.at[3])

    @pl.when(x % 2 == 1)
    def _():
        wait_bytes(pieces.at[0, pl.ds(HALF, ROWS - HALF)], send_k.at[3])

    wait_bytes(pieces.at[0], send_e)
    @pl.when(between)
    def _():
        wait_bytes(tiles.at[pl.ds(0, 6)], send_a.at[0])
        wait_bytes(sums, send_u)

    @pl.when(jnp.logical_not(between))
    def _():
        wait_bytes(tiles.at[pl.ds(0, 7)], send_a.at[0])

    @pl.when(jnp.logical_not(middle))
    def _():
        wait_bytes(tiles.at[0], send_a.at[1])

    for r in (0, 1):
        inside = rows_of[r] == blk

        @pl.when(inside)
        def _():
            wait_bytes(landed.at[pl.ds(0, 31)], send_b.at[r])

        @pl.when(jnp.logical_not(inside))
        def _():
            wait_bytes(landed.at[pl.ds(0, 32)], send_b.at[r])


def local(inputs, inducing):
    dma = pltpu.SemaphoreType.DMA
    regular = pltpu.SemaphoreType.REGULAR
    return pl.pallas_call(
        kernel,
        out_shape=jax.ShapeDtypeStruct((4, FEAT), jnp.float32),
        in_specs=[pl.BlockSpec(memory_space=pl.ANY)] * 2,
        out_specs=pl.BlockSpec(memory_space=pltpu.VMEM),
        scratch_shapes=[
            pltpu.VMEM((ROWS, FEAT), jnp.bfloat16),
            pltpu.VMEM((BLOCK, FEAT), jnp.bfloat16),
            pltpu.VMEM((6, ROWS, BLOCK), jnp.bfloat16),
            pltpu.VMEM((HALF, BLOCK), jnp.bfloat16),
            pltpu.VMEM((9, BLOCK, BLOCK), jnp.float32),
            pltpu.VMEM((2, 8, BLOCK, BLOCK), jnp.float32),
            pltpu.VMEM((2, BLOCK, BLOCK), jnp.float32),
            pltpu.VMEM((2, 32, 4, BLOCK), jnp.float32),
            pltpu.VMEM((64, 4, BLOCK), jnp.float32),
            dma((CHUNKS + 1,)),
            dma((4,)),
            dma((4,)),
            dma,
            dma((PASSED,)),
            dma((CHUNKS,)),
            dma,
            dma((2,)),
            dma((3,)),
            dma,
            dma((2,)),
            dma,
            regular,
            regular,
            regular,
        ],
        compiler_params=pltpu.CompilerParams(
            collective_id=0, has_side_effects=True, vmem_limit_bytes=215 * 256 * 1024
        ),
    )(inputs, inducing)


def solution(mesh):
    placed = (P("dp", None), P("blk", None))
    return jax.shard_map(
        local, mesh=mesh, in_specs=placed, out_specs=P(("blk", "dp"), None), check_vma=False
    )
```

```python
import jax
import jax.numpy as jnp
from jax import lax
from jax.experimental import pallas as pl
from jax.experimental.pallas import tpu as pltpu
from jax.sharding import PartitionSpec as P

ROWS = 1024
FEAT = 2048
BLOCK = 128
CUTS = (0, 128, 256, 640, 1024)
CHUNKS = len(CUTS) - 1
PASSED = 2
HALF = CUTS[PASSED]
TOTAL = 32768
OWN, EDGE, SIDE, FAR = 0, 2, 4, 5


def kernel(
    inputs, inducing, out, x_buf, i_buf, pieces, passing, tiles, parts, sums, strips, landed,
    in_sem, send_k, recv_k, send_p, recv_p, recv_e, send_e, send_a, recv_a, send_u, send_b, recv_b,
    round_p, round_z, round_w,
):
    blk, dp = lax.axis_index("blk"), lax.axis_index("dp")
    x, yh, c = blk // 4, blk // 2 % 2, blk % 2
    z, yl = dp // 2, dp % 2

    def block_of(x_, yh_, c_):
        return (x_ + 8) % 4 * 4 + yh_ * 2 + c_

    def group_of(z_, yl_):
        return (z_ + 32) % 16 * 2 + yl_

    def remote(src, dst, send, recv, device):
        return pltpu.make_async_remote_copy(
            src_ref=src, dst_ref=dst, send_sem=send, recv_sem=recv,
            device_id=device, device_id_type=pl.DeviceIdType.MESH,
        )

    def signal(sem, device):
        pl.semaphore_signal(sem, inc=1, device_id=device, device_id_type=pl.DeviceIdType.MESH)

    def wait_bytes(ref, sem):
        pltpu.make_async_copy(ref, ref, sem).wait()

    partner = (block_of(x, yh, 1 - c), dp)
    edge = (block_of(x, 1 - yh, c), dp)
    across = (block_of(x, 1 - yh, 1 - c), dp)
    beside = (blk, group_of(z, 1 - yl))
    line = [(block_of(x + s, yh, c), dp) for s in (1, 2, 3)]
    column = [(blk, group_of(z + s, l)) for s in (-2, -1, 1, 2) for l in (0, 1)]
    plane = [partner, edge, across] + line
    near = plane + [beside] + column
    barrier = pltpu.get_barrier_semaphore()
    for device in near:
        signal(barrier, device)

    load_i = pltpu.make_async_copy(inducing, i_buf, in_sem.at[CHUNKS])
    load_i.start()
    loads = []
    for n in range(CHUNKS):
        rows = pl.ds(CUTS[n], CUTS[n + 1] - CUTS[n])
        load = pltpu.make_async_copy(inputs.at[rows], x_buf.at[rows], in_sem.at[n])
        load.start()
        loads.append(load)

    def make_chunk(n):
        rows = pl.ds(CUTS[n], CUTS[n + 1] - CUTS[n])
        loads[n].wait()
        products = lax.dot_general(
            x_buf[rows, :], i_buf[...], (((1,), (1,)), ((), ())),
            preferred_element_type=jnp.float32,
        )
        pieces[OWN + c, rows, :] = (products * products * (1.0 / FEAT)).astype(jnp.bfloat16)

    def send_chunk(n):
        rows = pl.ds(CUTS[n], CUTS[n + 1] - CUTS[n])
        own = pieces.at[OWN + c, rows]
        remote(own, pieces.at[OWN + c, rows], send_k.at[0], recv_k.at[0], partner).start()
        remote(own, pieces.at[SIDE, rows], send_k.at[1], recv_k.at[1], line[2]).start()
        remote(own, pieces.at[EDGE + c, rows], send_k.at[2], recv_e.at[n], edge).start()

        if n < PASSED:

            @pl.when(x % 2 == 1)
            def _():
                remote(own, passing.at[rows], send_p, recv_p.at[n], line[0]).start()

    def send_far():
        @pl.when(x % 2 == 0)
        def _():
            remote(pieces.at[OWN + c], pieces.at[FAR], send_k.at[3], recv_k.at[2], line[1]).start()
            for n in range(PASSED):
                rows = pl.ds(CUTS[n], CUTS[n + 1] - CUTS[n])
                wait_bytes(passing.at[rows], recv_p.at[n])
                remote(passing.at[rows], pieces.at[FAR, rows], send_p, recv_k.at[2], line[0]).start()

        @pl.when(x % 2 == 1)
        def _():
            wait_bytes(pieces.at[0], send_k.at[1])
            rows = pl.ds(HALF, ROWS - HALF)
            remote(
                pieces.at[OWN + c, rows], pieces.at[FAR, rows], send_k.at[3], recv_k.at[2], line[1]
            ).start()

    load_i.wait()
    make_chunk(0)
    pl.semaphore_wait(barrier, len(near))
    send_chunk(0)
    for device in plane:
        signal(round_p, device)
    for n in range(1, CHUNKS):
        make_chunk(n)
        send_chunk(n)

    pl.semaphore_wait(round_p, len(plane))
    for s in (-2, 2):
        signal(round_z, (blk, group_of(z + s, yl)))

    def gram(left, *rights):
        turned = pieces[left].T
        return [
            lax.dot_general(
                turned, pieces[right], (((1,), (0,)), ((), ())),
                preferred_element_type=jnp.float32,
            )
            for right in rights
        ]

    reach = 1 + c
    meets = (yl + c + 1) % 2
    middle = z % 4 == 2 * c

    def send_tile(k, place):
        step = (k + 2 * c - z + 16 + reach) % 4 - reach
        if k == 0:
            target = group_of(z + step, yl)
            dst = parts.at[meets * place + 1 - meets, (meets * yl + (1 - meets) * place) * 4 + step + reach]
            recv = recv_a.at[meets * place + (1 - meets) * 2]
        else:
            target = group_of(z + step, (k // 4 + c) % 2)
            dst, recv = parts.at[0, yl * 4 + step + reach], recv_a.at[0]
        src = tiles.at[8 if place else k]

        @pl.when(target == dp)
        def _():
            pltpu.make_async_copy(src, dst, recv).start()

        @pl.when(target != dp)
        def _():
            remote(src, dst, send_a.at[place], recv, (blk, target)).start()

    wait_bytes(pieces.at[0], recv_k.at[0])
    tiles[0], tiles[8] = gram(OWN + c, OWN, OWN + 1)
    send_tile(0, 0)
    send_tile(0, 1)

    send_far()

    for n in range(CHUNKS):
        rows = pl.ds(CUTS[n], CUTS[n + 1] - CUTS[n])
        arrived = pieces.at[EDGE + c, rows]
        wait_bytes(arrived, recv_e.at[n])
        remote(arrived, arrived, send_e, recv_k.at[3], partner).start()

    pl.semaphore_wait(round_z, 2)
    for s in (-4, 4):
        signal(round_w, (blk, group_of(z + s, yl)))

    wait_bytes(pieces.at[0], recv_k.at[1])
    tiles[2], tiles[7] = gram(SIDE, OWN, OWN + 1)
    send_tile(2, 0)
    send_tile(7, 0)
    (tiles[5],) = gram(EDGE + c, OWN + (c + yh) % 2)
    send_tile(5, 0)

    wait_bytes(pieces.at[0], recv_k.at[3])
    tiles[4], tiles[1] = gram(SIDE, EDGE, EDGE + 1)
    send_tile(4, 0)
    send_tile(1, 0)

    between = jnp.logical_and(middle, meets == 0)

    @pl.when(between)
    def _():
        wait_bytes(parts.at[1], recv_a.at[2])
        for place in (0, 1):
            sums[place] = (
                parts[1, place * 4] + parts[1, place * 4 + 1]
                + parts[1, place * 4 + 2] + parts[1, place * 4 + 3]
            )
            remote(
                sums.at[place], parts.at[place, (1 - c) * 4], send_u, recv_a.at[place], beside
            ).start()

    wait_bytes(pieces.at[0], recv_k.at[2])
    half = (c + x // 2) % 2
    tiles[6], tiles[3] = gram(FAR, OWN + half, EDGE + half)
    send_tile(6, 0)
    send_tile(3, 0)

    pl.semaphore_wait(round_w, 2)

    mine = (yl + c) % 2 * 4 + (z + 2 * c) % 4
    first = mine == 0

    def one(k, value):
        return jnp.where(mine == k, value, 0)

    own_0, own_1 = block_of(x, yh, 0), block_of(x, yh, 1)
    edge_0, edge_1 = block_of(x, 1 - yh, 0), block_of(x, 1 - yh, 1)
    side, far = block_of(x + 1, yh, c), block_of(x + 2, yh, c)
    row = (
        one(0, blk) + one(2, side) + one(7, side) + one(4, side) + one(1, side)
        + one(5, block_of(x, 1 - yh, c)) + one(6, far) + one(3, far)
    )
    col = (
        one(0, own_0) + one(2, own_0) + one(7, own_1) + one(4, edge_0) + one(1, edge_1)
        + one(5, block_of(x, yh, (c + yh) % 2)) + one(6, block_of(x, yh, half))
        + one(3, block_of(x, 1 - yh, half))
    )
    rows_of = (row, jnp.where(first, blk, col))
    cols_of = (col, jnp.where(first, own_1, row))

    def add_parts(place, slots):
        total = parts[place, slots[0]]
        for s in slots[1:]:
            total = total + parts[place, s]
        return total * (1.0 / TOTAL)

    def lay(place, value):
        for s in range(32):
            strips[place, s] = value[4 * s : 4 * s + 4]

    @pl.when(first)
    def _():
        for place in (0, 1):
            wait_bytes(parts.at[place, pl.ds(0, 5)], recv_a.at[place])
            lay(place, add_parts(place, [(1 - c) * 4] + [c * 4 + s for s in range(4)]))

    @pl.when(jnp.logical_not(first))
    def _():
        wait_bytes(parts.at[0], recv_a.at[0])
        tile = add_parts(0, range(8))
        lay(0, tile)
        lay(1, tile.T)

    def send_strips(n, carry):
        w = n + n // 8 * (23 - 2 * n)
        for l in (0, 1):
            for r in (0, 1):
                src = strips.at[r, w * 2 + l]
                dst = landed.at[z // 4 * 16 + cols_of[r]]
                target = w * 2 + l
                here = jnp.logical_and(target == dp, rows_of[r] == blk)

                @pl.when(here)
                def _():
                    pltpu.make_async_copy(src, dst, recv_b).start()

                @pl.when(jnp.logical_not(here))
                def _():
                    remote(src, dst, send_b.at[r], recv_b, (rows_of[r], target)).start()

        return carry

    lax.fori_loop(0, 16, send_strips, 0)

    wait_bytes(landed, recv_b)
    for g in range(16):
        out[:, g * BLOCK : (g + 1) * BLOCK] = (
            landed[g] + landed[16 + g] + landed[32 + g] + landed[48 + g]
        )

    for n in (0, 2):
        wait_bytes(pieces.at[0], send_k.at[n])
    wait_bytes(passing, send_p)

    @pl.when(x % 2 == 0)
    def _():
        wait_bytes(pieces.at[0], send_k.at[1])
        wait_bytes(pieces.at[0], send_k.at[3])

    @pl.when(x % 2 == 1)
    def _():
        wait_bytes(pieces.at[0, pl.ds(HALF, ROWS - HALF)], send_k.at[3])

    wait_bytes(pieces.at[0], send_e)
    @pl.when(between)
    def _():
        wait_bytes(tiles.at[pl.ds(0, 6)], send_a.at[0])
        wait_bytes(sums, send_u)

    @pl.when(jnp.logical_not(between))
    def _():
        wait_bytes(tiles.at[pl.ds(0, 7)], send_a.at[0])

    @pl.when(jnp.logical_not(middle))
    def _():
        wait_bytes(tiles.at[0], send_a.at[1])

    for r in (0, 1):
        inside = rows_of[r] == blk

        @pl.when(inside)
        def _():
            wait_bytes(landed.at[pl.ds(0, 31)], send_b.at[r])

        @pl.when(jnp.logical_not(inside))
        def _():
            wait_bytes(landed.at[pl.ds(0, 32)], send_b.at[r])


def local(inputs, inducing):
    dma = pltpu.SemaphoreType.DMA
    regular = pltpu.SemaphoreType.REGULAR
    return pl.pallas_call(
        kernel,
        out_shape=jax.ShapeDtypeStruct((4, FEAT), jnp.float32),
        in_specs=[pl.BlockSpec(memory_space=pl.ANY)] * 2,
        out_specs=pl.BlockSpec(memory_space=pltpu.VMEM),
        scratch_shapes=[
            pltpu.VMEM((ROWS, FEAT), jnp.bfloat16),
            pltpu.VMEM((BLOCK, FEAT), jnp.bfloat16),
            pltpu.VMEM((6, ROWS, BLOCK), jnp.bfloat16),
            pltpu.VMEM((HALF, BLOCK), jnp.bfloat16),
            pltpu.VMEM((9, BLOCK, BLOCK), jnp.float32),
            pltpu.VMEM((2, 8, BLOCK, BLOCK), jnp.float32),
            pltpu.VMEM((2, BLOCK, BLOCK), jnp.float32),
            pltpu.VMEM((2, 32, 4, BLOCK), jnp.float32),
            pltpu.VMEM((64, 4, BLOCK), jnp.float32),
            dma((CHUNKS + 1,)),
            dma((4,)),
            dma((4,)),
            dma,
            dma((PASSED,)),
            dma((CHUNKS,)),
            dma,
            dma((2,)),
            dma((3,)),
            dma,
            dma((2,)),
            dma,
            regular,
            regular,
            regular,
        ],
        compiler_params=pltpu.CompilerParams(
            collective_id=0, has_side_effects=True, vmem_limit_bytes=215 * 256 * 1024
        ),
    )(inputs, inducing)


def solution(mesh):
    placed = (P("dp", None), P("blk", None))
    return jax.shard_map(
        local, mesh=mesh, in_specs=placed, out_specs=P(("blk", "dp"), None), check_vma=False
    )
```
